512 devices in a mesh: section: 16 (over y, core), tensor: 32 (over x, z).
Axes of the slice: x: 4, y: 8, z: 8, core: 2. Of those that a mesh axis runs over, the one named last changes fastest.
Arguments:
- carry_in: bfloat16 [16, 2, 64, 4096], P('section', None, 'tensor'), may hold values from -6 to 6
- norm_gain: float32 [16, 4096], P('section'), may hold values from 0.5 to 1.5
- w_gate: bfloat16 [16, 1536, 128, 128], P('section', 'tensor'), may hold values from -0.15625 to 0.15625
- w_up: bfloat16 [16, 1536, 128, 128], P('section', 'tensor'), may hold values from -0.15625 to 0.15625
- w_down: bfloat16 [16, 1536, 128, 128], P('section', 'tensor'), may hold values from -0.078125 to 0.078125
- tile_list: int32 [16, 1536], P('section', 'tensor'), may hold values from 0 to 128, as said below
- grad_in: bfloat16 [16, 2, 64, 4096], P('section', None, 'tensor'), may hold values from -6 to 6
Outputs:
- section_out: bfloat16 [16, 2, 64, 4096], P('section', None, 'tensor')
- grad_back: bfloat16 [16, 2, 64, 4096], P('section', None, 'tensor')
The draws below stay inside these ranges and needn't reach their ends.
Inputs may be any that keep to these rules, and one draw needn't show every extreme that they name: `tile_list`: for each layer and tensor index t, entries 48 * t to 48 * t + 47 list distinct tile numbers f * 32 + c (f a block of that device's hidden units, c a block of features) in rising order, followed by the padding value 4 * 32. Each such list has at least 24 live entries, and in every layer some tensor index has all 48 live.
All inputs are finite; a program needn't handle non-finite values.
Results may differ from the reference program's by a relative error of at most 0.013.
Values may be sent and summed in bfloat16 or wider, within the bound.
No kernel may reach another device: no remote copies, remote signals or barrier semaphores. Data moves between devices by JAX's collectives and lax.ppermute only.
A program may use at most 64 MiB of HBM per device.

```python
import jax
import jax.numpy as jnp
from jax import lax

D = 4096
BLK = 128
FB_DEV = 4
SLOTS = 48
MB = 2
TOK = 64
N_SECTION = 16
N_TENSOR = 32


def draw_tile_list(key, part):
    key_order = jax.random.fold_in(key, 11)
    key_count = jax.random.fold_in(key, 23)
    key_busy = jax.random.fold_in(key, 37)
    grid = FB_DEV * (D // BLK)
    scores = jax.random.randint(key_order, (N_SECTION, N_TENSOR, grid), 0, 1 << 20)
    cells = jnp.arange(grid, dtype=jnp.int32)
    ranked = jnp.argsort(scores * grid + cells[None, None, :], axis=-1)[:, :, :SLOTS]
    ranked = jnp.sort(ranked.astype(jnp.int32), axis=-1)
    counts = jax.random.randint(key_count, (N_SECTION, N_TENSOR), SLOTS // 2, SLOTS + 1)
    busiest = jax.random.randint(key_busy, (N_SECTION,), 0, N_TENSOR)
    devices = jnp.arange(N_TENSOR, dtype=jnp.int32)
    counts = jnp.where(devices[None, :] == busiest[:, None], SLOTS, counts)
    slots = jnp.arange(SLOTS, dtype=jnp.int32)
    listed = jnp.where(slots[None, None, :] < counts[:, :, None], ranked, grid)
    return listed.reshape(N_SECTION, N_TENSOR * SLOTS).astype(jnp.int32)


def shard_levels(own_key, dims, cuts, low, high):
    def one(position, blocks):
        draws = jax.random.uniform(jax.random.fold_in(jax.random.fold_in(own_key, 6), position), (blocks,), jnp.float32, low / len(cuts), high / len(cuts))
        return jnp.repeat(jnp.exp(draws), dims[position] // blocks).reshape((-1,) + (1,) * (len(dims) - position - 1))

    loudness = one(*cuts[0])
    for cut in cuts[1:]:
        loudness = loudness * one(*cut)
    return loudness


def bell_draw(rng, extent, deviation, reach, split=(), kind=jnp.bfloat16):
    level = shard_levels(rng, extent, split, -0.22, 0.18) if split else 1.0
    array = jax.random.normal(rng, extent, jnp.float32) * deviation * level
    return jnp.minimum(jnp.maximum(array, -reach), reach).astype(kind)


def setup_inputs(seed: int = 0) -> dict:
    splits = jax.random.split(jax.random.key(seed), 8)
    return {
        "carry_in": bell_draw(splits[0], (N_SECTION, MB, TOK, D), 1.0, 6.0, ((0, 16), (2, 32))),
        "norm_gain": jnp.clip(1.0 + 0.1 * jax.random.normal(splits[1], (N_SECTION, D), jnp.float32), 0.5, 1.5),
        "w_gate": bell_draw(splits[2], (N_SECTION, N_TENSOR * SLOTS, BLK, BLK), (BLK * SLOTS // FB_DEV) ** -0.5, 0.15625, ((0, 16), (1, 32))),
        "w_up": bell_draw(splits[3], (N_SECTION, N_TENSOR * SLOTS, BLK, BLK), (BLK * SLOTS // FB_DEV) ** -0.5, 0.15625, ((0, 16), (1, 32))),
        "w_down": bell_draw(splits[4], (N_SECTION, N_TENSOR * SLOTS, BLK, BLK), (max(BLK, BLK * N_TENSOR * SLOTS // (D // BLK))) ** -0.5, 0.078125, ((0, 16), (1, 32))),
        "tile_list": draw_tile_list(jax.random.fold_in(splits[7], 71), 0),
        "grad_in": bell_draw(splits[6], (N_SECTION, MB, TOK, D), 1.0, 6.0, ((0, 16), (2, 32))),
    }


EPS = 1e-05
HIGH = lax.Precision.HIGHEST

def tile_tables(tile_ids, fblocks, dblocks):
    live = tile_ids < fblocks * dblocks
    safe = jnp.where(live, tile_ids, 0).astype(jnp.int32)
    f_of = safe // dblocks
    d_of = safe - f_of * dblocks
    pick_f = jnp.logical_and(f_of[:, None] == jnp.arange(fblocks, dtype=jnp.int32)[None, :], live[:, None])
    pick_d = jnp.logical_and(d_of[:, None] == jnp.arange(dblocks, dtype=jnp.int32)[None, :], live[:, None])
    return (pick_f.astype(jnp.float32), pick_d.astype(jnp.float32))

def rms_scale(values):
    return lax.rsqrt(lax.optimization_barrier(jnp.mean(values * values, axis=-1, keepdims=True)) + EPS)

def ein(form, left, right):
    return jnp.einsum(form, left.astype(jnp.float32), right.astype(jnp.float32), precision=HIGH)

def one_section(section_args):
    x_in, gain, gate_tiles, up_tiles, down_tiles, tile_ids, grad_out = section_args
    dblocks = D // BLK
    rows = x_in.reshape(MB * TOK, D)
    scale = rms_scale(rows)
    normed = (rows * scale * gain).astype(jnp.bfloat16).reshape(MB * TOK, dblocks, BLK)
    grad_rows = grad_out.reshape(MB * TOK, dblocks, BLK)
    gate_tiles = gate_tiles.reshape(N_TENSOR, SLOTS, BLK, BLK)
    up_tiles = up_tiles.reshape(N_TENSOR, SLOTS, BLK, BLK)
    down_tiles = down_tiles.reshape(N_TENSOR, SLOTS, BLK, BLK)
    tile_ids = tile_ids.reshape(N_TENSOR, SLOTS)

    def one_device(carry, device_args):
        ffn_total, back_total = carry
        gate_w, up_w, down_w, ids_here = device_args
        pick_f, pick_d = tile_tables(ids_here, FB_DEV, dblocks)
        chosen = ein('rdc,kd->rkc', normed, pick_d)
        gate = ein('rke,kf->rfe', ein('rkc,kce->rke', chosen, gate_w), pick_f)
        up_proj = ein('rke,kf->rfe', ein('rkc,kce->rke', chosen, up_w), pick_f)
        hidden = (jax.nn.silu(gate) * up_proj).astype(jnp.bfloat16)
        spread = ein('rfc,kf->rkc', hidden, pick_f)
        term = ein('rke,kd->rde', ein('rkc,kce->rke', spread, down_w), pick_d)
        term = lax.optimization_barrier(term.astype(jnp.bfloat16)).astype(jnp.float32)
        picked = ein('rde,kd->rke', grad_rows, pick_d)
        d_hidden = ein('rkc,kf->rfc', ein('rke,kce->rkc', picked, down_w), pick_f)
        sigmoid_gate = jax.nn.sigmoid(gate)
        d_gate = (d_hidden * up_proj * sigmoid_gate * (1.0 + gate * (1.0 - sigmoid_gate))).astype(jnp.bfloat16)
        d_up = (d_hidden * gate * sigmoid_gate).astype(jnp.bfloat16)
        gate_spread = ein('rfe,kf->rke', d_gate, pick_f)
        up_spread = ein('rfe,kf->rke', d_up, pick_f)
        inner = ein('rke,kce->rkc', gate_spread, gate_w) + ein('rke,kce->rkc', up_spread, up_w)
        back = ein('rkc,kd->rdc', inner, pick_d)
        back = lax.optimization_barrier(back.astype(jnp.bfloat16)).astype(jnp.float32)
        return ((ffn_total + term, back_total + back), None)
    empty = jnp.zeros((MB * TOK, dblocks, BLK), jnp.float32)
    (ffn_total, back_total), _ = lax.scan(one_device, (empty, empty), (gate_tiles, up_tiles, down_tiles, tile_ids))
    ffn_total = ffn_total.reshape(MB * TOK, D)
    grad_normed = back_total.reshape(MB * TOK, D)
    output = (rows + ffn_total).astype(jnp.bfloat16)
    mixed = lax.optimization_barrier(jnp.mean(rows * gain * grad_normed, axis=-1, keepdims=True))
    grad_x = grad_out.reshape(MB * TOK, D).astype(jnp.float32) + scale * gain * grad_normed - rows * scale ** 3 * mixed
    return (output.reshape(MB, TOK, D), grad_x.astype(jnp.bfloat16).reshape(MB, TOK, D))

def reference(carry_in, norm_gain, w_gate, w_up, w_down, tile_list, grad_in):
    x_all = jnp.roll(carry_in, 1, axis=0).astype(jnp.float32)
    outputs, grads = lax.map(one_section, (x_all, norm_gain.astype(jnp.float32), w_gate, w_up, w_down, tile_list, grad_in))
    return (outputs, jnp.roll(grads, -1, axis=0))
```

```python
import jax
import jax.numpy as jnp
from jax import lax
from jax.experimental import pallas as pl
from jax.experimental.pallas import tpu as pltpu
from jax.sharding import PartitionSpec as P

EPS = 1e-05
BLK = 128
FB_DEV = 4
NX = 4
NZ = 8
ROWS = 4
F32 = jnp.float32
BF16 = jnp.bfloat16

ALONG_X = [[x * NZ + z for x in range(NX)] for z in range(NZ)]
ALONG_Z = [[x * NZ + z for z in range(NZ)] for x in range(NX)]


def shifted(block, axis, distance):
    devices = range(lax.axis_size(axis))
    route = [((i - distance) % len(devices), i) for i in devices]
    return lax.ppermute(block, axis, route)


def rms_scale(values):
    return lax.rsqrt(jnp.mean(values * values, axis=-1, keepdims=True) + EPS)


def exchange(chunks, groups):
    return lax.all_to_all(chunks, "tensor", 0, 0, axis_index_groups=groups)


def spread(shard, groups):
    copies = jnp.broadcast_to(shard[None], (len(groups[0]),) + shard.shape)
    return exchange(copies, groups)


def collected(chunks, groups):
    return jnp.sum(exchange(chunks, groups).astype(F32), axis=0)


def dot_t(left, right):
    return lax.dot_general(left, right, (((1,), (1,)), ((), ())), preferred_element_type=F32)


def layer_kernel(ids, g_ref, wg_ref, wu_ref, wd_ref, out_ref, xs, ds, gu, dh, hid, dgu, fo, bo):
    rows, width = g_ref.shape
    half = rows // 2
    dblocks = width // BLK
    slots = wg_ref.shape[0]
    live_ids = FB_DEV * dblocks

    row = lax.broadcasted_iota(jnp.int32, (rows, rows), 0)
    col = lax.broadcasted_iota(jnp.int32, (rows, rows), 1)

    def source(i):
        within = i % half
        return (within // ROWS) * (2 * ROWS) + within % ROWS + (i // half) * ROWS

    sort_rows = (col == source(row)).astype(BF16)
    mix_rows = (row == source(col)).astype(BF16)

    for k in range(width // (2 * BLK)):
        part = jnp.dot(
            sort_rows, g_ref[:, k * 2 * BLK : (k + 1) * 2 * BLK], preferred_element_type=F32
        ).astype(BF16)
        for i in range(2):
            xs[2 * k + i] = part[:half, i * BLK : (i + 1) * BLK]
            ds[2 * k + i] = part[half:, i * BLK : (i + 1) * BLK]
    xs[dblocks] = jnp.zeros((half, BLK), BF16)
    ds[dblocks] = jnp.zeros((half, BLK), BF16)
    gu[...] = jnp.zeros_like(gu)
    dh[...] = jnp.zeros_like(dh)
    fo[...] = jnp.zeros_like(fo)
    bo[...] = jnp.zeros_like(bo)

    def place(j):
        q = ids[j]
        live = q < live_ids
        return jnp.where(live, q // dblocks, 0), jnp.where(live, q % dblocks, dblocks)

    def inward(j, carry):
        h, c = place(j)
        w = jnp.concatenate([wg_ref[j], wu_ref[j]], axis=1)
        gu[h] += jnp.dot(xs[c], w, preferred_element_type=F32)
        dh[h] += dot_t(ds[c], wd_ref[j])
        return carry

    lax.fori_loop(0, slots, inward, 0, unroll=8)

    for h in range(FB_DEV):
        gate = gu[h, :, :BLK]
        up = gu[h, :, BLK:]
        sig = 1.0 / (1.0 + jnp.exp(-gate))
        hid[h] = (gate * sig * up).astype(BF16)
        d_hidden = dh[h]
        dgu[h, :, :BLK] = (d_hidden * up * sig * (1.0 + gate * (1.0 - sig))).astype(BF16)
        dgu[h, :, BLK:] = (d_hidden * gate * sig).astype(BF16)

    def outward(j, carry):
        h, c = place(j)
        w = jnp.concatenate([wg_ref[j], wu_ref[j]], axis=1)
        fo[c] += jnp.dot(hid[h], wd_ref[j], preferred_element_type=F32)
        bo[c] += dot_t(dgu[h], w)
        return carry

    lax.fori_loop(0, slots, outward, 0, unroll=8)

    for k in range(dblocks):
        both = jnp.concatenate([fo[k].astype(BF16), bo[k].astype(BF16)], axis=0)
        out_ref[:, k * BLK : (k + 1) * BLK] = jnp.dot(
            mix_rows, both, preferred_element_type=F32
        ).astype(BF16)


def layer(ids, gathered, w_gate, w_up, w_down):
    rows, width = gathered.shape
    half = rows // 2
    dblocks = width // BLK
    vmem = pl.BlockSpec(memory_space=pltpu.VMEM)
    slots = w_gate.shape[0]
    return pl.pallas_call(
        layer_kernel,
        out_shape=jax.ShapeDtypeStruct((rows, width), BF16),
        in_specs=[pl.BlockSpec(memory_space=pltpu.SMEM), vmem, vmem, vmem, vmem],
        out_specs=vmem,
        scratch_shapes=[
            pltpu.VMEM((dblocks + 1, half, BLK), BF16),
            pltpu.VMEM((dblocks + 1, half, BLK), BF16),
            pltpu.VMEM((FB_DEV, half, 2 * BLK), F32),
            pltpu.VMEM((FB_DEV, half, BLK), F32),
            pltpu.VMEM((FB_DEV, half, BLK), BF16),
            pltpu.VMEM((FB_DEV, half, 2 * BLK), BF16),
            pltpu.VMEM((dblocks + 1, half, BLK), F32),
            pltpu.VMEM((dblocks + 1, half, BLK), F32),
        ],
        compiler_params=pltpu.CompilerParams(vmem_limit_bytes=40 * 1024 * 1024),
        cost_estimate=pl.CostEstimate(
            flops=12 * slots * half * BLK * BLK,
            bytes_accessed=6 * slots * BLK * BLK + 4 * rows * width,
            transcendentals=FB_DEV * half * BLK,
        ),
    )(ids, gathered, w_gate, w_up, w_down)


def on_device(carry_in, norm_gain, w_gate, w_up, w_down, tile_list, grad_in):
    _, batches, tok_dev, width = carry_in.shape
    own = batches * tok_dev
    x_own = shifted(carry_in.reshape(own, width), "section", 1).astype(F32)
    dy_own = grad_in.reshape(own, width)
    gain = norm_gain[0]
    scale = rms_scale(x_own)
    normed = (x_own * scale * gain).astype(BF16)

    shard = jnp.concatenate([normed, dy_own], axis=0)
    gathered = spread(shard, ALONG_Z)
    gathered = spread(gathered.reshape(NZ * 2 * own, width), ALONG_X)
    gathered = gathered.reshape(NX * NZ * 2 * own, width)

    terms = layer(tile_list[0], gathered, w_gate[0], w_up[0], w_down[0])

    sums = collected(terms.reshape(NX, NZ * 2 * own, width), ALONG_X).astype(BF16)
    sums = collected(sums.reshape(NZ, 2 * own, width), ALONG_Z)
    ffn_own = sums[:own]
    grad_normed = sums[own:]

    section_out = (x_own + ffn_own).astype(BF16)
    mixed = jnp.mean(x_own * gain * grad_normed, axis=-1, keepdims=True)
    grad_x = dy_own.astype(F32) + scale * gain * grad_normed - x_own * scale**3 * mixed
    grad_back = shifted(grad_x.astype(BF16), "section", -1)
    return (
        section_out.reshape(1, batches, tok_dev, width),
        grad_back.reshape(1, batches, tok_dev, width),
    )


def solution(mesh):
    placed = (
        P("section", None, "tensor", None),
        P("section", None),
        P("section", "tensor", None, None),
        P("section", "tensor", None, None),
        P("section", "tensor", None, None),
        P("section", "tensor"),
        P("section", None, "tensor", None),
    )
    return jax.shard_map(
        on_device,
        mesh=mesh,
        in_specs=placed,
        out_specs=(P("section", None, "tensor", None), P("section", None, "tensor", None)),
        check_vma=False,
    )
```

```python
import jax
import jax.numpy as jnp
from jax import lax
from jax.experimental import pallas as pl
from jax.experimental.pallas import tpu as pltpu
from jax.sharding import PartitionSpec as P

EPS = 1e-05
BLK = 128
FB_DEV = 4
NX = 4
NZ = 8
ROWS = 4
F32 = jnp.float32
BF16 = jnp.bfloat16

SPARSE = [[x * NZ + z for z in range(p, NZ, 2)] for x in range(NX) for p in range(2)]
DENSE = [[x * NZ + z + p for x in range(NX) for p in range(2)] for z in range(0, NZ, 2)]


def shifted(block, axis, distance):
    devices = range(lax.axis_size(axis))
    route = [((i - distance) % len(devices), i) for i in devices]
    return lax.ppermute(block, axis, route)


def rms_scale(values):
    return lax.rsqrt(jnp.mean(values * values, axis=-1, keepdims=True) + EPS)


def exchange(chunks, groups):
    return lax.all_to_all(chunks, "tensor", 0, 0, axis_index_groups=groups)


def spread(shard, groups):
    copies = jnp.broadcast_to(shard[None], (len(groups[0]),) + shard.shape)
    return exchange(copies, groups)


def collected(chunks, groups):
    return jnp.sum(exchange(chunks, groups).astype(F32), axis=0)


def dot_t(left, right):
    return lax.dot_general(left, right, (((1,), (1,)), ((), ())), preferred_element_type=F32)


def layer_kernel(ids, g_ref, wg_ref, wu_ref, wd_ref, out_ref, xs, ds, gu, dh, hid, dgu, fo, bo):
    rows, width = g_ref.shape
    half = rows // 2
    dblocks = width // BLK
    slots = wg_ref.shape[0]
    live_ids = FB_DEV * dblocks

    row = lax.broadcasted_iota(jnp.int32, (rows, rows), 0)
    col = lax.broadcasted_iota(jnp.int32, (rows, rows), 1)

    def source(i):
        within = i % half
        return (within // ROWS) * (2 * ROWS) + within % ROWS + (i // half) * ROWS

    sort_rows = (col == source(row)).astype(BF16)
    mix_rows = (row == source(col)).astype(BF16)

    for k in range(width // (2 * BLK)):
        part = jnp.dot(
            sort_rows, g_ref[:, k * 2 * BLK : (k + 1) * 2 * BLK], preferred_element_type=F32
        ).astype(BF16)
        for i in range(2):
            xs[2 * k + i] = part[:half, i * BLK : (i + 1) * BLK]
            ds[2 * k + i] = part[half:, i * BLK : (i + 1) * BLK]
    xs[dblocks] = jnp.zeros((half, BLK), BF16)
    ds[dblocks] = jnp.zeros((half, BLK), BF16)
    gu[...] = jnp.zeros_like(gu)
    dh[...] = jnp.zeros_like(dh)
    fo[...] = jnp.zeros_like(fo)
    bo[...] = jnp.zeros_like(bo)

    def place(j):
        q = ids[j]
        live = q < live_ids
        return jnp.where(live, q // dblocks, 0), jnp.where(live, q % dblocks, dblocks)

    def inward(j, carry):
        h, c = place(j)
        w = jnp.concatenate([wg_ref[j], wu_ref[j]], axis=1)
        gu[h] += jnp.dot(xs[c], w, preferred_element_type=F32)
        dh[h] += dot_t(ds[c], wd_ref[j])
        return carry

    lax.fori_loop(0, slots, inward, 0, unroll=8)

    for h in range(FB_DEV):
        gate = gu[h, :, :BLK]
        up = gu[h, :, BLK:]
        sig = 1.0 / (1.0 + jnp.exp(-gate))
        hid[h] = (gate * sig * up).astype(BF16)
        d_hidden = dh[h]
        dgu[h, :, :BLK] = (d_hidden * up * sig * (1.0 + gate * (1.0 - sig))).astype(BF16)
        dgu[h, :, BLK:] = (d_hidden * gate * sig).astype(BF16)

    def outward(j, carry):
        h, c = place(j)
        w = jnp.concatenate([wg_ref[j], wu_ref[j]], axis=1)
        fo[c] += jnp.dot(hid[h], wd_ref[j], preferred_element_type=F32)
        bo[c] += dot_t(dgu[h], w)
        return carry

    lax.fori_loop(0, slots, outward, 0, unroll=8)

    for k in range(dblocks):
        both = jnp.concatenate([fo[k].astype(BF16), bo[k].astype(BF16)], axis=0)
        out_ref[:, k * BLK : (k + 1) * BLK] = jnp.dot(
            mix_rows, both, preferred_element_type=F32
        ).astype(BF16)


def layer(ids, gathered, w_gate, w_up, w_down):
    rows, width = gathered.shape
    half = rows // 2
    dblocks = width // BLK
    vmem = pl.BlockSpec(memory_space=pltpu.VMEM)
    slots = w_gate.shape[0]
    return pl.pallas_call(
        layer_kernel,
        out_shape=jax.ShapeDtypeStruct((rows, width), BF16),
        in_specs=[pl.BlockSpec(memory_space=pltpu.SMEM), vmem, vmem, vmem, vmem],
        out_specs=vmem,
        scratch_shapes=[
            pltpu.VMEM((dblocks + 1, half, BLK), BF16),
            pltpu.VMEM((dblocks + 1, half, BLK), BF16),
            pltpu.VMEM((FB_DEV, half, 2 * BLK), F32),
            pltpu.VMEM((FB_DEV, half, BLK), F32),
            pltpu.VMEM((FB_DEV, half, BLK), BF16),
            pltpu.VMEM((FB_DEV, half, 2 * BLK), BF16),
            pltpu.VMEM((dblocks + 1, half, BLK), F32),
            pltpu.VMEM((dblocks + 1, half, BLK), F32),
        ],
        compiler_params=pltpu.CompilerParams(vmem_limit_bytes=40 * 1024 * 1024),
        cost_estimate=pl.CostEstimate(
            flops=12 * slots * half * BLK * BLK,
            bytes_accessed=6 * slots * BLK * BLK + 4 * rows * width,
            transcendentals=FB_DEV * half * BLK,
        ),
    )(ids, gathered, w_gate, w_up, w_down)


def on_device(carry_in, norm_gain, w_gate, w_up, w_down, tile_list, grad_in):
    _, batches, tok_dev, width = carry_in.shape
    own = batches * tok_dev
    x_own = shifted(carry_in.reshape(own, width), "section", 1).astype(F32)
    dy_own = grad_in.reshape(own, width)
    gain = norm_gain[0]
    scale = rms_scale(x_own)
    normed = (x_own * scale * gain).astype(BF16)

    shard = jnp.concatenate([normed, dy_own], axis=0)
    gathered = spread(shard, SPARSE).reshape(-1, width)
    gathered = spread(gathered, DENSE).reshape(-1, width)

    terms = layer(tile_list[0], gathered, w_gate[0], w_up[0], w_down[0])

    sums = collected(terms.reshape(len(DENSE[0]), -1, width), DENSE).astype(BF16)
    sums = collected(sums.reshape(len(SPARSE[0]), -1, width), SPARSE)
    ffn_own = sums[:own]
    grad_normed = sums[own:]

    section_out = (x_own + ffn_own).astype(BF16)
    mixed = jnp.mean(x_own * gain * grad_normed, axis=-1, keepdims=True)
    grad_x = dy_own.astype(F32) + scale * gain * grad_normed - x_own * scale**3 * mixed
    grad_back = shifted(grad_x.astype(BF16), "section", -1)
    return (
        section_out.reshape(1, batches, tok_dev, width),
        grad_back.reshape(1, batches, tok_dev, width),
    )


def solution(mesh):
    placed = (
        P("section", None, "tensor", None),
        P("section", None),
        P("section", "tensor", None, None),
        P("section", "tensor", None, None),
        P("section", "tensor", None, None),
        P("section", "tensor"),
        P("section", None, "tensor", None),
    )
    return jax.shard_map(
        on_device,
        mesh=mesh,
        in_specs=placed,
        out_specs=(P("section", None, "tensor", None), P("section", None, "tensor", None)),
        check_vma=False,
    )
```

```python
import jax
import jax.numpy as jnp
from jax import lax
from jax.experimental import pallas as pl
from jax.experimental.pallas import tpu as pltpu
from jax.sharding import PartitionSpec as P

EPS = 1e-05
BLK = 128
FB_DEV = 4
NX = 4
NZ = 8
ROWS = 4
F32 = jnp.float32
BF16 = jnp.bfloat16

SPARSE = [
    [x * NZ + z for x in range(p, NX, 2) for z in range(q, NZ, 2)]
    for p in range(2)
    for q in range(2)
]
DENSE = [
    [(x + p) * NZ + z + q for p in range(2) for q in range(2)]
    for x in range(0, NX, 2)
    for z in range(0, NZ, 2)
]


def shifted(block, axis, distance):
    devices = range(lax.axis_size(axis))
    route = [((i - distance) % len(devices), i) for i in devices]
    return lax.ppermute(block, axis, route)


def rms_scale(values):
    return lax.rsqrt(jnp.mean(values * values, axis=-1, keepdims=True) + EPS)


def exchange(chunks, groups):
    return lax.all_to_all(chunks, "tensor", 0, 0, axis_index_groups=groups)


def spread(shard, groups):
    copies = jnp.broadcast_to(shard[None], (len(groups[0]),) + shard.shape)
    return exchange(copies, groups)


def collected(chunks, groups):
    return jnp.sum(exchange(chunks, groups).astype(F32), axis=0)


def dot_t(left, right):
    return lax.dot_general(left, right, (((1,), (1,)), ((), ())), preferred_element_type=F32)


def layer_kernel(ids, g_ref, wg_ref, wu_ref, wd_ref, out_ref, xs, ds, gu, dh, hid, dgu, fo, bo):
    rows, width = g_ref.shape
    half = rows // 2
    dblocks = width // BLK
    slots = wg_ref.shape[0]
    live_ids = FB_DEV * dblocks

    row = lax.broadcasted_iota(jnp.int32, (rows, rows), 0)
    col = lax.broadcasted_iota(jnp.int32, (rows, rows), 1)

    def source(i):
        within = i % half
        return (within // ROWS) * (2 * ROWS) + within % ROWS + (i // half) * ROWS

    sort_rows = (col == source(row)).astype(BF16)
    mix_rows = (row == source(col)).astype(BF16)

    for k in range(width // (2 * BLK)):
        part = jnp.dot(
            sort_rows, g_ref[:, k * 2 * BLK : (k + 1) * 2 * BLK], preferred_element_type=F32
        ).astype(BF16)
        for i in range(2):
            xs[2 * k + i] = part[:half, i * BLK : (i + 1) * BLK]
            ds[2 * k + i] = part[half:, i * BLK : (i + 1) * BLK]
    xs[dblocks] = jnp.zeros((half, BLK), BF16)
    ds[dblocks] = jnp.zeros((half, BLK), BF16)
    gu[...] = jnp.zeros_like(gu)
    dh[...] = jnp.zeros_like(dh)
    fo[...] = jnp.zeros_like(fo)
    bo[...] = jnp.zeros_like(bo)

    def place(j):
        q = ids[j]
        live = q < live_ids
        return jnp.where(live, q // dblocks, 0), jnp.where(live, q % dblocks, dblocks)

    def inward(j, carry):
        h, c = place(j)
        w = jnp.concatenate([wg_ref[j], wu_ref[j]], axis=1)
        gu[h] += jnp.dot(xs[c], w, preferred_element_type=F32)
        dh[h] += dot_t(ds[c], wd_ref[j])
        return carry

    lax.fori_loop(0, slots, inward, 0, unroll=8)

    for h in range(FB_DEV):
        gate = gu[h, :, :BLK]
        up = gu[h, :, BLK:]
        sig = 1.0 / (1.0 + jnp.exp(-gate))
        hid[h] = (gate * sig * up).astype(BF16)
        d_hidden = dh[h]
        dgu[h, :, :BLK] = (d_hidden * up * sig * (1.0 + gate * (1.0 - sig))).astype(BF16)
        dgu[h, :, BLK:] = (d_hidden * gate * sig).astype(BF16)

    def outward(j, carry):
        h, c = place(j)
        w = jnp.concatenate([wg_ref[j], wu_ref[j]], axis=1)
        fo[c] += jnp.dot(hid[h], wd_ref[j], preferred_element_type=F32)
        bo[c] += dot_t(dgu[h], w)
        return carry

    lax.fori_loop(0, slots, outward, 0, unroll=8)

    for k in range(dblocks):
        both = jnp.concatenate([fo[k].astype(BF16), bo[k].astype(BF16)], axis=0)
        out_ref[:, k * BLK : (k + 1) * BLK] = jnp.dot(
            mix_rows, both, preferred_element_type=F32
        ).astype(BF16)


def layer(ids, gathered, w_gate, w_up, w_down):
    rows, width = gathered.shape
    half = rows // 2
    dblocks = width // BLK
    vmem = pl.BlockSpec(memory_space=pltpu.VMEM)
    slots = w_gate.shape[0]
    return pl.pallas_call(
        layer_kernel,
        out_shape=jax.ShapeDtypeStruct((rows, width), BF16),
        in_specs=[pl.BlockSpec(memory_space=pltpu.SMEM), vmem, vmem, vmem, vmem],
        out_specs=vmem,
        scratch_shapes=[
            pltpu.VMEM((dblocks + 1, half, BLK), BF16),
            pltpu.VMEM((dblocks + 1, half, BLK), BF16),
            pltpu.VMEM((FB_DEV, half, 2 * BLK), F32),
            pltpu.VMEM((FB_DEV, half, BLK), F32),
            pltpu.VMEM((FB_DEV, half, BLK), BF16),
            pltpu.VMEM((FB_DEV, half, 2 * BLK), BF16),
            pltpu.VMEM((dblocks + 1, half, BLK), F32),
            pltpu.VMEM((dblocks + 1, half, BLK), F32),
        ],
        compiler_params=pltpu.CompilerParams(vmem_limit_bytes=40 * 1024 * 1024),
        cost_estimate=pl.CostEstimate(
            flops=12 * slots * half * BLK * BLK,
            bytes_accessed=6 * slots * BLK * BLK + 4 * rows * width,
            transcendentals=FB_DEV * half * BLK,
        ),
    )(ids, gathered, w_gate, w_up, w_down)


def on_device(carry_in, norm_gain, w_gate, w_up, w_down, tile_list, grad_in):
    _, batches, tok_dev, width = carry_in.shape
    own = batches * tok_dev
    x_own = shifted(carry_in.reshape(own, width), "section", 1).astype(F32)
    dy_own = grad_in.reshape(own, width)
    gain = norm_gain[0]
    scale = rms_scale(x_own)
    normed = (x_own * scale * gain).astype(BF16)

    shard = jnp.concatenate([normed, dy_own], axis=0)
    gathered = spread(shard, SPARSE).reshape(-1, width)
    gathered = spread(gathered, DENSE).reshape(-1, width)

    terms = layer(tile_list[0], gathered, w_gate[0], w_up[0], w_down[0])

    sums = collected(terms.reshape(len(DENSE[0]), -1, width), DENSE).astype(BF16)
    sums = collected(sums.reshape(len(SPARSE[0]), -1, width), SPARSE)
    ffn_own = sums[:own]
    grad_normed = sums[own:]

    section_out = (x_own + ffn_own).astype(BF16)
    mixed = jnp.mean(x_own * gain * grad_normed, axis=-1, keepdims=True)
    grad_x = dy_own.astype(F32) + scale * gain * grad_normed - x_own * scale**3 * mixed
    grad_back = shifted(grad_x.astype(BF16), "section", -1)
    return (
        section_out.reshape(1, batches, tok_dev, width),
        grad_back.reshape(1, batches, tok_dev, width),
    )


def solution(mesh):
    placed = (
        P("section", None, "tensor", None),
        P("section", None),
        P("section", "tensor", None, None),
        P("section", "tensor", None, None),
        P("section", "tensor", None, None),
        P("section", "tensor"),
        P("section", None, "tensor", None),
    )
    return jax.shard_map(
        on_device,
        mesh=mesh,
        in_specs=placed,
        out_specs=(P("section", None, "tensor", None), P("section", None, "tensor", None)),
        check_vma=False,
    )
```

```python
import jax
import jax.numpy as jnp
from jax import lax
from jax.experimental import pallas as pl
from jax.experimental.pallas import tpu as pltpu
from jax.sharding import PartitionSpec as P

EPS = 1e-05
BLK = 128
FB_DEV = 4
DBLOCKS = 32
NX = 4
NZ = 8
F32 = jnp.float32
BF16 = jnp.bfloat16
VMEM = pl.BlockSpec(memory_space=pltpu.VMEM)
SMEM = pl.BlockSpec(memory_space=pltpu.SMEM)
STEP = 512

SPARSE = [[x * NZ + z for z in range(p, NZ, 2)] for x in range(NX) for p in range(2)]
DENSE = [[x * NZ + z + p for x in range(NX) for p in range(2)] for z in range(0, NZ, 2)]
N_SPARSE = len(SPARSE[0])
N_DENSE = len(DENSE[0])


def shifted(block, axis, distance):
    devices = range(lax.axis_size(axis))
    route = [((i - distance) % len(devices), i) for i in devices]
    return lax.ppermute(block, axis, route)


def exchange(chunks, groups):
    return lax.all_to_all(chunks, "tensor", 0, 0, axis_index_groups=groups)


def dot(left, right):
    return jnp.dot(left, right, preferred_element_type=F32)


def dot_t(left, right):
    return lax.dot_general(left, right, (((1,), (1,)), ((), ())), preferred_element_type=F32)


def own_rows(ref):
    return jnp.concatenate([ref[0, i].astype(F32) for i in range(ref.shape[1])], axis=0)


def rms_scale(values):
    return lax.rsqrt(jnp.mean(values * values, axis=-1, keepdims=True) + EPS)


def call(kernel, out, *args, specs=None, scratch=(), **kwargs):
    return pl.pallas_call(
        kernel,
        out_shape=out,
        in_specs=specs or [VMEM] * len(args),
        out_specs=jax.tree.map(lambda _: VMEM, out),
        scratch_shapes=scratch,
        **kwargs,
    )(*args)


def shard_kernel(x_ref, dy_ref, gain_ref, out_ref):
    x = own_rows(x_ref)
    shard = jnp.concatenate([x * rms_scale(x) * gain_ref[...], own_rows(dy_ref)], axis=0)
    for i in range(out_ref.shape[0]):
        out_ref[i] = shard.astype(BF16)


def regroup(rows, own, forward):
    shards = rows // (2 * own)
    i = lax.broadcasted_iota(jnp.int32, (rows, rows), 0)
    j = lax.broadcasted_iota(jnp.int32, (rows, rows), 1)
    k = i if forward else j
    other = j if forward else i
    array, within = k // (shards * own), k % (shards * own)
    return (other == (within // own) * 2 * own + array * own + within % own).astype(BF16)


def spread_kernel(in_ref, out_ref):
    rows, width = in_ref.shape
    order = regroup(rows, rows // (2 * N_SPARSE), True)
    for k in range(0, width, STEP):
        part = dot(order, in_ref[:, k : k + STEP]).astype(BF16)
        for i in range(out_ref.shape[0]):
            out_ref[i, :, k : k + STEP] = part


def collect_kernel(in_ref, out_ref):
    rows, width = out_ref.shape
    order = regroup(rows, rows // (2 * N_SPARSE), False)
    for k in range(0, width, STEP):
        total = in_ref[0, :, k : k + STEP].astype(F32)
        for i in range(1, in_ref.shape[0]):
            total += in_ref[i, :, k : k + STEP].astype(F32)
        out_ref[:, k : k + STEP] = dot(order, total.astype(BF16)).astype(BF16)


def final_kernel(sums_ref, x_ref, dy_ref, gain_ref, out_ref, grad_ref):
    total = sums_ref[0].astype(F32)
    for i in range(1, sums_ref.shape[0]):
        total += sums_ref[i].astype(F32)
    own = total.shape[0] // 2
    x = own_rows(x_ref)
    gain = gain_ref[...]
    scale = rms_scale(x)
    grad_normed = total[own:]
    mixed = jnp.mean(x * gain * grad_normed, axis=-1, keepdims=True)
    grad_x = own_rows(dy_ref) + scale * gain * grad_normed - x * (scale * scale * scale) * mixed
    section_out = x + total[:own]
    tok = out_ref.shape[2]
    for i in range(out_ref.shape[1]):
        out_ref[0, i] = section_out[i * tok : (i + 1) * tok].astype(BF16)
        grad_ref[0, i] = grad_x[i * tok : (i + 1) * tok].astype(BF16)


def pair_kernel(ids, table):
    slots, = ids.shape
    pairs = table.shape[0]

    @pl.loop(0, pairs)
    def _(p):
        table[p, 0] = 0
        table[p, 1] = 0
        table[p, 2] = FB_DEV
        table[p, 3] = DBLOCKS
        table[p, 4] = DBLOCKS

    def take(i, carry):
        p, last, odd = carry
        q = ids[i]
        h = q // DBLOCKS
        c = q % DBLOCKS
        second = jnp.logical_and(h == last, odd == 1)
        p = jnp.where(second, p, p + 1)

        @pl.when(jnp.logical_and(q < FB_DEV * DBLOCKS, jnp.logical_not(second)))
        def _():
            table[p, 0] = i
            table[p, 1] = i
            table[p, 2] = h
            table[p, 3] = c

        @pl.when(jnp.logical_and(q < FB_DEV * DBLOCKS, second))
        def _():
            table[p, 1] = i
            table[p, 4] = c

        return p, h, jnp.where(second, 0, 1)

    lax.fori_loop(0, slots, take, (jnp.int32(-1), jnp.int32(-1), jnp.int32(0)))


def layer_kernel(table, g_ref, wg_ref, wu_ref, wd_ref, out_ref, gu, dh, hid, dgu, fo, bo):
    members, height, width = g_ref.shape
    half = height // 2
    rows = members * half
    dblocks = width // BLK
    pairs = table.shape[0]

    gu[...] = jnp.zeros_like(gu)
    dh[...] = jnp.zeros_like(dh)
    fo[...] = jnp.zeros_like(fo)
    bo[...] = jnp.zeros_like(bo)

    def columns(first, c):
        at = pl.ds(pl.multiple_of(jnp.minimum(c, dblocks - 1) * BLK, BLK), BLK)
        block = g_ref[:, first : first + half, at].reshape(rows, BLK)
        return jnp.where(c < dblocks, block, jnp.zeros_like(block))

    def tiles(ref, a, b, axis):
        return jnp.concatenate([ref[a], ref[b]], axis=axis)

    def both(a, b):
        return jnp.concatenate([tiles(wg_ref, a, b, 0), tiles(wu_ref, a, b, 0)], axis=1)

    for p in range(pairs):
        a, b, h, ca, cb = [table[p, i] for i in range(5)]
        x = jnp.concatenate([columns(0, ca), columns(0, cb)], axis=1)
        dy = jnp.concatenate([columns(half, ca), columns(half, cb)], axis=1)
        gu[h] += dot(x, both(a, b))
        dh[h] += dot_t(dy, tiles(wd_ref, a, b, 1))

    for h in range(FB_DEV):
        gate = gu[h, :, :BLK]
        up = gu[h, :, BLK:]
        sig = 1.0 / (1.0 + jnp.exp(-gate))
        hid[h] = (gate * sig * up).astype(BF16)
        d_hidden = dh[h]
        dgu[h, :, :BLK] = (d_hidden * up * sig * (1.0 + gate * (1.0 - sig))).astype(BF16)
        dgu[h, :, BLK:] = (d_hidden * gate * sig).astype(BF16)
    hid[FB_DEV] = jnp.zeros_like(hid[FB_DEV])
    dgu[FB_DEV] = jnp.zeros_like(dgu[FB_DEV])

    for p in range(pairs):
        a, b, h, ca, cb = [table[p, i] for i in range(5)]
        forth = dot(hid[h], tiles(wd_ref, a, b, 1))
        back = dot_t(dgu[h], both(a, b))
        fo[ca] += forth[:, :BLK]
        fo[cb] += forth[:, BLK:]
        bo[ca] += back[:, :BLK]
        bo[cb] += back[:, BLK:]

    for k in range(dblocks):
        at = slice(k * BLK, (k + 1) * BLK)
        out_ref[:, :half, at] = fo[k].astype(BF16).reshape(members, half, BLK)
        out_ref[:, half:, at] = bo[k].astype(BF16).reshape(members, half, BLK)


def pair_table(ids):
    slots, = ids.shape
    pairs = (slots + FB_DEV) // 2
    return pl.pallas_call(
        pair_kernel,
        out_shape=jax.ShapeDtypeStruct((pairs, 8), jnp.int32),
        in_specs=[SMEM],
        out_specs=SMEM,
    )(ids)


def layer(table, gathered, w_gate, w_up, w_down):
    members, height, width = gathered.shape
    rows = members * height // 2
    dblocks = width // BLK
    slots = w_gate.shape[0]
    return call(
        layer_kernel,
        jax.ShapeDtypeStruct(gathered.shape, BF16),
        table,
        gathered,
        w_gate,
        w_up,
        w_down,
        specs=[SMEM] + [VMEM] * 4,
        scratch=[
            pltpu.VMEM((FB_DEV + 1, rows, 2 * BLK), F32),
            pltpu.VMEM((FB_DEV + 1, rows, BLK), F32),
            pltpu.VMEM((FB_DEV + 1, rows, BLK), BF16),
            pltpu.VMEM((FB_DEV + 1, rows, 2 * BLK), BF16),
            pltpu.VMEM((dblocks + 1, rows, BLK), F32),
            pltpu.VMEM((dblocks + 1, rows, BLK), F32),
        ],
        compiler_params=pltpu.CompilerParams(vmem_limit_bytes=40 * 1024 * 1024),
        cost_estimate=pl.CostEstimate(
            flops=12 * slots * rows * BLK * BLK,
            bytes_accessed=6 * slots * BLK * BLK + 8 * rows * width,
            transcendentals=FB_DEV * rows * BLK,
        ),
    )


def on_device(carry_in, norm_gain, w_gate, w_up, w_down, tile_list, grad_in):
    own = carry_in.shape[1] * carry_in.shape[2]
    width = carry_in.shape[3]
    x_own = shifted(carry_in, "section", 1)
    table = pair_table(tile_list[0])

    copies = jax.ShapeDtypeStruct((N_SPARSE, 2 * own, width), BF16)
    shards = call(shard_kernel, copies, x_own, grad_in, norm_gain)
    shards = exchange(shards, SPARSE).reshape(-1, width)
    copies = jax.ShapeDtypeStruct((N_DENSE,) + shards.shape, BF16)
    gathered = exchange(call(spread_kernel, copies, shards), DENSE)

    terms = layer(table, gathered, w_gate[0], w_up[0], w_down[0])

    sums = call(
        collect_kernel, jax.ShapeDtypeStruct(shards.shape, BF16), exchange(terms, DENSE)
    )
    sums = exchange(sums.reshape(N_SPARSE, -1, width), SPARSE)
    like = jax.ShapeDtypeStruct(carry_in.shape, BF16)
    section_out, grad_x = call(final_kernel, (like, like), sums, x_own, grad_in, norm_gain)
    return section_out, shifted(grad_x, "section", -1)


def solution(mesh):
    placed = (
        P("section", None, "tensor", None),
        P("section", None),
        P("section", "tensor", None, None),
        P("section", "tensor", None, None),
        P("section", "tensor", None, None),
        P("section", "tensor"),
        P("section", None, "tensor", None),
    )
    return jax.shard_map(
        on_device,
        mesh=mesh,
        in_specs=placed,
        out_specs=(P("section", None, "tensor", None), P("section", None, "tensor", None)),
        check_vma=False,
    )
```

```python
import jax
import jax.numpy as jnp
from jax import lax
from jax.experimental import pallas as pl
from jax.experimental.pallas import tpu as pltpu
from jax.sharding import PartitionSpec as P

EPS = 1e-05
BLK = 128
FB_DEV = 4
DBLOCKS = 32
NX = 4
NZ = 8
ROWS = 4
F32 = jnp.float32
BF16 = jnp.bfloat16

SPARSE = [[x * NZ + z for z in range(p, NZ, 2)] for x in range(NX) for p in range(2)]
DENSE = [[x * NZ + z + p for x in range(NX) for p in range(2)] for z in range(0, NZ, 2)]


def shifted(block, axis, distance):
    devices = range(lax.axis_size(axis))
    route = [((i - distance) % len(devices), i) for i in devices]
    return lax.ppermute(block, axis, route)


def rms_scale(values):
    return lax.rsqrt(jnp.mean(values * values, axis=-1, keepdims=True) + EPS)


def exchange(chunks, groups):
    return lax.all_to_all(chunks, "tensor", 0, 0, axis_index_groups=groups)


def spread(shard, groups):
    copies = jnp.broadcast_to(shard[None], (len(groups[0]),) + shard.shape)
    return exchange(copies, groups)


def collected(chunks, groups):
    return jnp.sum(exchange(chunks, groups).astype(F32), axis=0)


def dot_t(left, right):
    return lax.dot_general(left, right, (((1,), (1,)), ((), ())), preferred_element_type=F32)


def pair_kernel(ids, table):
    slots, = ids.shape
    pairs = table.shape[0]

    @pl.loop(0, pairs)
    def _(p):
        table[p, 0] = 0
        table[p, 1] = 0
        table[p, 2] = FB_DEV
        table[p, 3] = DBLOCKS
        table[p, 4] = DBLOCKS

    def take(i, carry):
        p, last, odd = carry
        q = ids[i]
        h = q // DBLOCKS
        c = q % DBLOCKS
        second = jnp.logical_and(h == last, odd == 1)
        p = jnp.where(second, p, p + 1)

        @pl.when(jnp.logical_and(q < FB_DEV * DBLOCKS, jnp.logical_not(second)))
        def _():
            table[p, 0] = i
            table[p, 1] = i
            table[p, 2] = h
            table[p, 3] = c

        @pl.when(jnp.logical_and(q < FB_DEV * DBLOCKS, second))
        def _():
            table[p, 1] = i
            table[p, 4] = c

        return p, h, jnp.where(second, 0, 1)

    lax.fori_loop(0, slots, take, (jnp.int32(-1), jnp.int32(-1), jnp.int32(0)))


def layer_kernel(table, g_ref, wg_ref, wu_ref, wd_ref, out_ref, xs, ds, gu, dh, hid, dgu, fo, bo):
    rows, width = g_ref.shape
    half = rows // 2
    pairs = table.shape[0]

    row = lax.broadcasted_iota(jnp.int32, (rows, rows), 0)
    col = lax.broadcasted_iota(jnp.int32, (rows, rows), 1)

    def source(i):
        within = i % half
        return (within // ROWS) * (2 * ROWS) + within % ROWS + (i // half) * ROWS

    sort_rows = (col == source(row)).astype(BF16)
    mix_rows = (row == source(col)).astype(BF16)

    gu[...] = jnp.zeros_like(gu)
    dh[...] = jnp.zeros_like(dh)
    fo[...] = jnp.zeros_like(fo)
    bo[...] = jnp.zeros_like(bo)
    for k in range(width // (2 * BLK)):
        part = jnp.dot(
            sort_rows, g_ref[:, k * 2 * BLK : (k + 1) * 2 * BLK], preferred_element_type=F32
        ).astype(BF16)
        for i in range(2):
            xs[2 * k + i] = part[:half, i * BLK : (i + 1) * BLK]
            ds[2 * k + i] = part[half:, i * BLK : (i + 1) * BLK]
    xs[DBLOCKS] = jnp.zeros((half, BLK), BF16)
    ds[DBLOCKS] = jnp.zeros((half, BLK), BF16)

    def tiles(ref, a, b, axis):
        return jnp.concatenate([ref[a], ref[b]], axis=axis)

    def both(a, b):
        return jnp.concatenate([tiles(wg_ref, a, b, 0), tiles(wu_ref, a, b, 0)], axis=1)

    for p in range(pairs):
        a, b, h, ca, cb = [table[p, i] for i in range(5)]
        gu[h] += jnp.dot(tiles(xs, ca, cb, 1), both(a, b), preferred_element_type=F32)
        dh[h] += dot_t(tiles(ds, ca, cb, 1), tiles(wd_ref, a, b, 1))

    for h in range(FB_DEV):
        gate = gu[h, :, :BLK]
        up = gu[h, :, BLK:]
        sig = 1.0 / (1.0 + jnp.exp(-gate))
        hid[h] = (gate * sig * up).astype(BF16)
        d_hidden = dh[h]
        dgu[h, :, :BLK] = (d_hidden * up * sig * (1.0 + gate * (1.0 - sig))).astype(BF16)
        dgu[h, :, BLK:] = (d_hidden * gate * sig).astype(BF16)
    hid[FB_DEV] = jnp.zeros((half, BLK), BF16)
    dgu[FB_DEV] = jnp.zeros((half, 2 * BLK), BF16)

    for p in range(pairs):
        a, b, h, ca, cb = [table[p, i] for i in range(5)]
        forth = jnp.dot(hid[h], tiles(wd_ref, a, b, 1), preferred_element_type=F32)
        back = dot_t(dgu[h], both(a, b))
        fo[ca] += forth[:, :BLK]
        fo[cb] += forth[:, BLK:]
        bo[ca] += back[:, :BLK]
        bo[cb] += back[:, BLK:]

    for k in range(DBLOCKS // 2):
        terms = [
            jnp.concatenate([fo[i].astype(BF16), bo[i].astype(BF16)], axis=0)
            for i in (2 * k, 2 * k + 1)
        ]
        out_ref[:, k * 2 * BLK : (k + 1) * 2 * BLK] = jnp.dot(
            mix_rows, jnp.concatenate(terms, axis=1), preferred_element_type=F32
        ).astype(BF16)


def pair_table(ids):
    slots, = ids.shape
    pairs = (slots + FB_DEV) // 2
    return pl.pallas_call(
        pair_kernel,
        out_shape=jax.ShapeDtypeStruct((pairs, 8), jnp.int32),
        in_specs=[pl.BlockSpec(memory_space=pltpu.SMEM)],
        out_specs=pl.BlockSpec(memory_space=pltpu.SMEM),
    )(ids)


def layer(table, gathered, w_gate, w_up, w_down):
    rows, width = gathered.shape
    half = rows // 2
    dblocks = width // BLK
    vmem = pl.BlockSpec(memory_space=pltpu.VMEM)
    slots = w_gate.shape[0]
    return pl.pallas_call(
        layer_kernel,
        out_shape=jax.ShapeDtypeStruct((rows, width), BF16),
        in_specs=[pl.BlockSpec(memory_space=pltpu.SMEM), vmem, vmem, vmem, vmem],
        out_specs=vmem,
        scratch_shapes=[
            pltpu.VMEM((dblocks + 1, half, BLK), BF16),
            pltpu.VMEM((dblocks + 1, half, BLK), BF16),
            pltpu.VMEM((FB_DEV + 1, half, 2 * BLK), F32),
            pltpu.VMEM((FB_DEV + 1, half, BLK), F32),
            pltpu.VMEM((FB_DEV + 1, half, BLK), BF16),
            pltpu.VMEM((FB_DEV + 1, half, 2 * BLK), BF16),
            pltpu.VMEM((dblocks + 1, half, BLK), F32),
            pltpu.VMEM((dblocks + 1, half, BLK), F32),
        ],
        compiler_params=pltpu.CompilerParams(vmem_limit_bytes=40 * 1024 * 1024),
        cost_estimate=pl.CostEstimate(
            flops=12 * slots * half * BLK * BLK,
            bytes_accessed=6 * slots * BLK * BLK + 4 * rows * width,
            transcendentals=FB_DEV * half * BLK,
        ),
    )(table, gathered, w_gate, w_up, w_down)


def on_device(carry_in, norm_gain, w_gate, w_up, w_down, tile_list, grad_in):
    _, batches, tok_dev, width = carry_in.shape
    own = batches * tok_dev
    x_own = shifted(carry_in.reshape(own, width), "section", 1).astype(F32)
    dy_own = grad_in.reshape(own, width)
    gain = norm_gain[0]
    scale = rms_scale(x_own)
    normed = (x_own * scale * gain).astype(BF16)

    table, normed = lax.optimization_barrier((pair_table(tile_list[0]), normed))
    shard = jnp.concatenate([normed, dy_own], axis=0)
    gathered = spread(shard, SPARSE).reshape(-1, width)
    gathered = spread(gathered, DENSE).reshape(-1, width)

    terms = layer(table, gathered, w_gate[0], w_up[0], w_down[0])

    sums = collected(terms.reshape(len(DENSE[0]), -1, width), DENSE).astype(BF16)
    sums = collected(sums.reshape(len(SPARSE[0]), -1, width), SPARSE)
    ffn_own = sums[:own]
    grad_normed = sums[own:]

    section_out = (x_own + ffn_own).astype(BF16)
    mixed = jnp.mean(x_own * gain * grad_normed, axis=-1, keepdims=True)
    grad_x = dy_own.astype(F32) + scale * gain * grad_normed - x_own * scale**3 * mixed
    grad_back = shifted(grad_x.astype(BF16), "section", -1)
    return (
        section_out.reshape(1, batches, tok_dev, width),
        grad_back.reshape(1, batches, tok_dev, width),
    )


def solution(mesh):
    placed = (
        P("section", None, "tensor", None),
        P("section", None),
        P("section", "tensor", None, None),
        P("section", "tensor", None, None),
        P("section", "tensor", None, None),
        P("section", "tensor"),
        P("section", None, "tensor", None),
    )
    return jax.shard_map(
        on_device,
        mesh=mesh,
        in_specs=placed,
        out_specs=(P("section", None, "tensor", None), P("section", None, "tensor", None)),
        check_vma=False,
    )
```

```python
import jax
import jax.numpy as jnp
from jax import lax
from jax.experimental import pallas as pl
from jax.experimental.pallas import tpu as pltpu
from jax.sharding import PartitionSpec as P

EPS = 1e-05
BLK = 128
FB_DEV = 4
DBLOCKS = 32
NX = 4
NZ = 8
ROWS = 4
F32 = jnp.float32
BF16 = jnp.bfloat16

SPARSE = [[x * NZ + z for z in range(p, NZ, 2)] for x in range(NX) for p in range(2)]
DENSE = [[x * NZ + z + p for x in range(NX) for p in range(2)] for z in range(0, NZ, 2)]


def shifted(block, axis, distance):
    devices = range(lax.axis_size(axis))
    route = [((i - distance) % len(devices), i) for i in devices]
    return lax.ppermute(block, axis, route)


def rms_scale(values):
    return lax.rsqrt(jnp.mean(values * values, axis=-1, keepdims=True) + EPS)


def exchange(chunks, groups):
    return lax.all_to_all(chunks, "tensor", 0, 0, axis_index_groups=groups)


def spread(shard, groups):
    copies = jnp.broadcast_to(shard[None], (len(groups[0]),) + shard.shape)
    return exchange(copies, groups)


def collected(chunks, groups):
    return jnp.sum(exchange(chunks, groups).astype(F32), axis=0)


def dot_t(left, right):
    return lax.dot_general(left, right, (((1,), (1,)), ((), ())), preferred_element_type=F32)


def fill_pairs(ids, table):
    slots, = ids.shape
    pairs = table.shape[0] - 1
    for p in range(pairs):
        table[p] = packed(0, 0, FB_DEV, DBLOCKS, DBLOCKS)
    p = jnp.int32(-1)
    last = jnp.int32(-1)
    first = jnp.int32(0)
    first_c = jnp.int32(0)
    open_pair = jnp.bool_(False)
    for i in range(slots):
        q = ids[i]
        h = q // DBLOCKS
        c = q % DBLOCKS
        live = h < FB_DEV
        joins = jnp.logical_and(open_pair, h == last)
        p = jnp.where(joins, p, p + 1)
        first = jnp.where(joins, first, i)
        first_c = jnp.where(joins, first_c, c)
        table[jnp.where(live, p, pairs)] = packed(
            first, i, h, first_c, jnp.where(joins, c, DBLOCKS)
        )
        open_pair = jnp.logical_not(joins)
        last = h


def packed(a, b, h, ca, cb):
    return (((h * 64 + ca) * 64 + cb) * 64 + a) * 64 + b


def unpacked(word):
    return (word // 64) % 64, word % 64, word // 64**4, (word // 64**3) % 64, (word // 64**2) % 64


def layer_kernel(ids, g_ref, wg_ref, wu_ref, wd_ref, out_ref, table, xs, ds, gu, dh, hid, dgu, fo, bo):
    rows, width = g_ref.shape
    half = rows // 2
    pairs = table.shape[0] - 1
    fill_pairs(ids, table)

    row = lax.broadcasted_iota(jnp.int32, (rows, rows), 0)
    col = lax.broadcasted_iota(jnp.int32, (rows, rows), 1)

    def source(i):
        within = i % half
        return (within // ROWS) * (2 * ROWS) + within % ROWS + (i // half) * ROWS

    sort_rows = (col == source(row)).astype(BF16)
    mix_rows = (row == source(col)).astype(BF16)

    gu[...] = jnp.zeros_like(gu)
    dh[...] = jnp.zeros_like(dh)
    fo[...] = jnp.zeros_like(fo)
    bo[...] = jnp.zeros_like(bo)
    for k in range(width // (2 * BLK)):
        part = jnp.dot(
            sort_rows, g_ref[:, k * 2 * BLK : (k + 1) * 2 * BLK], preferred_element_type=F32
        ).astype(BF16)
        for i in range(2):
            xs[2 * k + i] = part[:half, i * BLK : (i + 1) * BLK]
            ds[2 * k + i] = part[half:, i * BLK : (i + 1) * BLK]
    xs[DBLOCKS] = jnp.zeros((half, BLK), BF16)
    ds[DBLOCKS] = jnp.zeros((half, BLK), BF16)

    def tiles(ref, a, b, axis):
        return jnp.concatenate([ref[a], ref[b]], axis=axis)

    def both(a, b):
        return jnp.concatenate([tiles(wg_ref, a, b, 0), tiles(wu_ref, a, b, 0)], axis=1)

    for p in range(pairs):
        a, b, h, ca, cb = unpacked(table[p])
        gu[h] += jnp.dot(tiles(xs, ca, cb, 1), both(a, b), preferred_element_type=F32)
        dh[h] += dot_t(tiles(ds, ca, cb, 1), tiles(wd_ref, a, b, 1))

    for h in range(FB_DEV):
        gate = gu[h, :, :BLK]
        up = gu[h, :, BLK:]
        sig = 1.0 / (1.0 + jnp.exp(-gate))
        hid[h] = (gate * sig * up).astype(BF16)
        d_hidden = dh[h]
        dgu[h, :, :BLK] = (d_hidden * up * sig * (1.0 + gate * (1.0 - sig))).astype(BF16)
        dgu[h, :, BLK:] = (d_hidden * gate * sig).astype(BF16)
    hid[FB_DEV] = jnp.zeros((half, BLK), BF16)
    dgu[FB_DEV] = jnp.zeros((half, 2 * BLK), BF16)

    for p in range(pairs):
        a, b, h, ca, cb = unpacked(table[p])
        forth = jnp.dot(hid[h], tiles(wd_ref, a, b, 1), preferred_element_type=F32)
        back = dot_t(dgu[h], both(a, b))
        fo[ca] += forth[:, :BLK]
        fo[cb] += forth[:, BLK:]
        bo[ca] += back[:, :BLK]
        bo[cb] += back[:, BLK:]

    for k in range(DBLOCKS // 2):
        terms = [
            jnp.concatenate([fo[i].astype(BF16), bo[i].astype(BF16)], axis=0)
            for i in (2 * k, 2 * k + 1)
        ]
        out_ref[:, k * 2 * BLK : (k + 1) * 2 * BLK] = jnp.dot(
            mix_rows, jnp.concatenate(terms, axis=1), preferred_element_type=F32
        ).astype(BF16)


def layer(ids, gathered, w_gate, w_up, w_down):
    rows, width = gathered.shape
    half = rows // 2
    dblocks = width // BLK
    vmem = pl.BlockSpec(memory_space=pltpu.VMEM)
    slots = w_gate.shape[0]
    return pl.pallas_call(
        layer_kernel,
        out_shape=jax.ShapeDtypeStruct((rows, width), BF16),
        in_specs=[pl.BlockSpec(memory_space=pltpu.SMEM), vmem, vmem, vmem, vmem],
        out_specs=vmem,
        scratch_shapes=[
            pltpu.SMEM(((slots + FB_DEV) // 2 + 1,), jnp.int32),
            pltpu.VMEM((dblocks + 1, half, BLK), BF16),
            pltpu.VMEM((dblocks + 1, half, BLK), BF16),
            pltpu.VMEM((FB_DEV + 1, half, 2 * BLK), F32),
            pltpu.VMEM((FB_DEV + 1, half, BLK), F32),
            pltpu.VMEM((FB_DEV + 1, half, BLK), BF16),
            pltpu.VMEM((FB_DEV + 1, half, 2 * BLK), BF16),
            pltpu.VMEM((dblocks + 1, half, BLK), F32),
            pltpu.VMEM((dblocks + 1, half, BLK), F32),
        ],
        compiler_params=pltpu.CompilerParams(vmem_limit_bytes=40 * 1024 * 1024),
        cost_estimate=pl.CostEstimate(
            flops=12 * slots * half * BLK * BLK,
            bytes_accessed=6 * slots * BLK * BLK + 4 * rows * width,
            transcendentals=FB_DEV * half * BLK,
        ),
    )(ids, gathered, w_gate, w_up, w_down)


def on_device(carry_in, norm_gain, w_gate, w_up, w_down, tile_list, grad_in):
    _, batches, tok_dev, width = carry_in.shape
    own = batches * tok_dev
    x_own = shifted(carry_in.reshape(own, width), "section", 1).astype(F32)
    dy_own = grad_in.reshape(own, width)
    gain = norm_gain[0]
    scale = rms_scale(x_own)
    normed = (x_own * scale * gain).astype(BF16)

    shard = jnp.concatenate([normed, dy_own], axis=0)
    gathered = spread(shard, SPARSE).reshape(-1, width)
    gathered = spread(gathered, DENSE).reshape(-1, width)

    terms = layer(tile_list[0], gathered, w_gate[0], w_up[0], w_down[0])

    sums = collected(terms.reshape(len(DENSE[0]), -1, width), DENSE).astype(BF16)
    sums = collected(sums.reshape(len(SPARSE[0]), -1, width), SPARSE)
    ffn_own = sums[:own]
    grad_normed = sums[own:]

    section_out = (x_own + ffn_own).astype(BF16)
    mixed = jnp.mean(x_own * gain * grad_normed, axis=-1, keepdims=True)
    grad_x = dy_own.astype(F32) + scale * gain * grad_normed - x_own * scale**3 * mixed
    grad_back = shifted(grad_x.astype(BF16), "section", -1)
    return (
        section_out.reshape(1, batches, tok_dev, width),
        grad_back.reshape(1, batches, tok_dev, width),
    )


def solution(mesh):
    placed = (
        P("section", None, "tensor", None),
        P("section", None),
        P("section", "tensor", None, None),
        P("section", "tensor", None, None),
        P("section", "tensor", None, None),
        P("section", "tensor"),
        P("section", None, "tensor", None),
    )
    return jax.shard_map(
        on_device,
        mesh=mesh,
        in_specs=placed,
        out_specs=(P("section", None, "tensor", None), P("section", None, "tensor", None)),
        check_vma=False,
    )
```

```python
import jax
import jax.numpy as jnp
from jax import lax
from jax.experimental import pallas as pl
from jax.experimental.pallas import tpu as pltpu
from jax.sharding import PartitionSpec as P

EPS = 1e-05
BLK = 128
FB_DEV = 4
DBLOCKS = 32
NX = 4
NZ = 8
ROWS = 4
F32 = jnp.float32
BF16 = jnp.bfloat16

FIRST = (
    [[x * NZ + z for z in range(NZ)] for x in range(NX)],
    [[x * NZ + z + p for x in range(NX) for p in range(2)] for z in range(0, NZ, 2)],
)
LAST = (
    [[x * NZ + z for x in range(NX)] for z in range(NZ)],
    [[x * NZ + z for z in range(p, NZ, 2)] for x in range(NX) for p in range(2)],
)


def shifted(block, axis, distance):
    devices = range(lax.axis_size(axis))
    route = [((i - distance) % len(devices), i) for i in devices]
    return lax.ppermute(block, axis, route)


def rms_scale(values):
    return lax.rsqrt(jnp.mean(values * values, axis=-1, keepdims=True) + EPS)


def exchange(chunks, ways):
    tensor = lax.axis_size("tensor")
    groups = [
        [section * tensor + i for i in group]
        for section in range(lax.axis_size("section"))
        for group in ways[section % 2]
    ]
    return lax.all_to_all(chunks, ("section", "tensor"), 0, 0, axis_index_groups=groups)


def spread(shard, ways):
    copies = jnp.broadcast_to(shard[None], (len(ways[0][0]),) + shard.shape)
    return exchange(copies, ways)


def collected(chunks, ways):
    return jnp.sum(exchange(chunks, ways).astype(F32), axis=0)


def dot_t(left, right):
    return lax.dot_general(left, right, (((1,), (1,)), ((), ())), preferred_element_type=F32)


def fill_pairs(ids, table):
    slots, = ids.shape
    pairs = table.shape[0] - 1
    for p in range(pairs):
        table[p] = packed(0, 0, FB_DEV, DBLOCKS, DBLOCKS)
    p = jnp.int32(-1)
    last = jnp.int32(-1)
    first = jnp.int32(0)
    first_c = jnp.int32(0)
    open_pair = jnp.bool_(False)
    for i in range(slots):
        q = ids[i]
        h = q // DBLOCKS
        c = q % DBLOCKS
        live = h < FB_DEV
        joins = jnp.logical_and(open_pair, h == last)
        p = jnp.where(joins, p, p + 1)
        first = jnp.where(joins, first, i)
        first_c = jnp.where(joins, first_c, c)
        table[jnp.where(live, p, pairs)] = packed(
            first, i, h, first_c, jnp.where(joins, c, DBLOCKS)
        )
        open_pair = jnp.logical_not(joins)
        last = h


def packed(a, b, h, ca, cb):
    return (((h * 64 + ca) * 64 + cb) * 64 + a) * 64 + b


def unpacked(word):
    return (word // 64) % 64, word % 64, word // 64**4, (word // 64**3) % 64, (word // 64**2) % 64


def layer_kernel(ids, g_ref, wg_ref, wu_ref, wd_ref, out_ref, table, xs, ds, gu, dh, hid, dgu, fo, bo):
    rows, width = g_ref.shape
    half = rows // 2
    pairs = table.shape[0] - 1
    fill_pairs(ids, table)

    row = lax.broadcasted_iota(jnp.int32, (rows, rows), 0)
    col = lax.broadcasted_iota(jnp.int32, (rows, rows), 1)

    def source(i):
        within = i % half
        return (within // ROWS) * (2 * ROWS) + within % ROWS + (i // half) * ROWS

    sort_rows = (col == source(row)).astype(BF16)
    mix_rows = (row == source(col)).astype(BF16)

    gu[...] = jnp.zeros_like(gu)
    dh[...] = jnp.zeros_like(dh)
    fo[...] = jnp.zeros_like(fo)
    bo[...] = jnp.zeros_like(bo)
    for k in range(width // (2 * BLK)):
        part = jnp.dot(
            sort_rows, g_ref[:, k * 2 * BLK : (k + 1) * 2 * BLK], preferred_element_type=F32
        ).astype(BF16)
        for i in range(2):
            xs[2 * k + i] = part[:half, i * BLK : (i + 1) * BLK]
            ds[2 * k + i] = part[half:, i * BLK : (i + 1) * BLK]
    xs[DBLOCKS] = jnp.zeros((half, BLK), BF16)
    ds[DBLOCKS] = jnp.zeros((half, BLK), BF16)

    def tiles(ref, a, b, axis):
        return jnp.concatenate([ref[a], ref[b]], axis=axis)

    def both(a, b):
        return jnp.concatenate([tiles(wg_ref, a, b, 0), tiles(wu_ref, a, b, 0)], axis=1)

    for p in range(pairs):
        a, b, h, ca, cb = unpacked(table[p])
        gu[h] += jnp.dot(tiles(xs, ca, cb, 1), both(a, b), preferred_element_type=F32)
        dh[h] += dot_t(tiles(ds, ca, cb, 1), tiles(wd_ref, a, b, 1))

    for h in range(FB_DEV):
        gate = gu[h, :, :BLK]
        up = gu[h, :, BLK:]
        sig = 1.0 / (1.0 + jnp.exp(-gate))
        hid[h] = (gate * sig * up).astype(BF16)
        d_hidden = dh[h]
        dgu[h, :, :BLK] = (d_hidden * up * sig * (1.0 + gate * (1.0 - sig))).astype(BF16)
        dgu[h, :, BLK:] = (d_hidden * gate * sig).astype(BF16)
    hid[FB_DEV] = jnp.zeros((half, BLK), BF16)
    dgu[FB_DEV] = jnp.zeros((half, 2 * BLK), BF16)

    for p in range(pairs):
        a, b, h, ca, cb = unpacked(table[p])
        forth = jnp.dot(hid[h], tiles(wd_ref, a, b, 1), preferred_element_type=F32)
        back = dot_t(dgu[h], both(a, b))
        fo[ca] += forth[:, :BLK]
        fo[cb] += forth[:, BLK:]
        bo[ca] += back[:, :BLK]
        bo[cb] += back[:, BLK:]

    for k in range(DBLOCKS // 2):
        terms = [
            jnp.concatenate([fo[i].astype(BF16), bo[i].astype(BF16)], axis=0)
            for i in (2 * k, 2 * k + 1)
        ]
        out_ref[:, k * 2 * BLK : (k + 1) * 2 * BLK] = jnp.dot(
            mix_rows, jnp.concatenate(terms, axis=1), preferred_element_type=F32
        ).astype(BF16)


def layer(ids, gathered, w_gate, w_up, w_down):
    rows, width = gathered.shape
    half = rows // 2
    dblocks = width // BLK
    vmem = pl.BlockSpec(memory_space=pltpu.VMEM)
    slots = w_gate.shape[0]
    return pl.pallas_call(
        layer_kernel,
        out_shape=jax.ShapeDtypeStruct((rows, width), BF16),
        in_specs=[pl.BlockSpec(memory_space=pltpu.SMEM), vmem, vmem, vmem, vmem],
        out_specs=vmem,
        scratch_shapes=[
            pltpu.SMEM(((slots + FB_DEV) // 2 + 1,), jnp.int32),
            pltpu.VMEM((dblocks + 1, half, BLK), BF16),
            pltpu.VMEM((dblocks + 1, half, BLK), BF16),
            pltpu.VMEM((FB_DEV + 1, half, 2 * BLK), F32),
            pltpu.VMEM((FB_DEV + 1, half, BLK), F32),
            pltpu.VMEM((FB_DEV + 1, half, BLK), BF16),
            pltpu.VMEM((FB_DEV + 1, half, 2 * BLK), BF16),
            pltpu.VMEM((dblocks + 1, half, BLK), F32),
            pltpu.VMEM((dblocks + 1, half, BLK), F32),
        ],
        compiler_params=pltpu.CompilerParams(vmem_limit_bytes=40 * 1024 * 1024),
        cost_estimate=pl.CostEstimate(
            flops=12 * slots * half * BLK * BLK,
            bytes_accessed=6 * slots * BLK * BLK + 4 * rows * width,
            transcendentals=FB_DEV * half * BLK,
        ),
    )(ids, gathered, w_gate, w_up, w_down)


def on_device(carry_in, norm_gain, w_gate, w_up, w_down, tile_list, grad_in):
    _, batches, tok_dev, width = carry_in.shape
    own = batches * tok_dev
    x_own = shifted(carry_in.reshape(own, width), "section", 1).astype(F32)
    dy_own = grad_in.reshape(own, width)
    gain = norm_gain[0]
    scale = rms_scale(x_own)
    normed = (x_own * scale * gain).astype(BF16)

    shard = jnp.concatenate([normed, dy_own], axis=0)
    gathered = spread(shard, FIRST).reshape(-1, width)
    gathered = spread(gathered, LAST).reshape(-1, width)

    terms = layer(tile_list[0], gathered, w_gate[0], w_up[0], w_down[0])

    sums = collected(terms.reshape(len(LAST[0][0]), -1, width), LAST).astype(BF16)
    sums = collected(sums.reshape(len(FIRST[0][0]), -1, width), FIRST)
    ffn_own = sums[:own]
    grad_normed = sums[own:]

    section_out = (x_own + ffn_own).astype(BF16)
    mixed = jnp.mean(x_own * gain * grad_normed, axis=-1, keepdims=True)
    grad_x = dy_own.astype(F32) + scale * gain * grad_normed - x_own * scale**3 * mixed
    grad_back = shifted(grad_x.astype(BF16), "section", -1)
    return (
        section_out.reshape(1, batches, tok_dev, width),
        grad_back.reshape(1, batches, tok_dev, width),
    )


def solution(mesh):
    placed = (
        P("section", None, "tensor", None),
        P("section", None),
        P("section", "tensor", None, None),
        P("section", "tensor", None, None),
        P("section", "tensor", None, None),
        P("section", "tensor"),
        P("section", None, "tensor", None),
    )
    return jax.shard_map(
        on_device,
        mesh=mesh,
        in_specs=placed,
        out_specs=(P("section", None, "tensor", None), P("section", None, "tensor", None)),
        check_vma=False,
    )
```

```python
import jax
import jax.numpy as jnp
from jax import lax
from jax.experimental import pallas as pl
from jax.experimental.pallas import tpu as pltpu
from jax.sharding import PartitionSpec as P

EPS = 1e-05
BLK = 128
FB_DEV = 4
DBLOCKS = 32
NX = 4
NZ = 8
ROWS = 4
F32 = jnp.float32
BF16 = jnp.bfloat16

SPARSE = [[x * NZ + z for z in range(p, NZ, 2)] for x in range(NX) for p in range(2)]
DENSE = [[x * NZ + z + p for x in range(NX) for p in range(2)] for z in range(0, NZ, 2)]


def shifted(block, axis, distance):
    devices = range(lax.axis_size(axis))
    route = [((i - distance) % len(devices), i) for i in devices]
    return lax.ppermute(block, axis, route)


def rms_scale(values):
    return lax.rsqrt(jnp.mean(values * values, axis=-1, keepdims=True) + EPS)


def exchange(chunks, groups):
    return lax.all_to_all(chunks, "tensor", 0, 0, axis_index_groups=groups)


def spread(shard, groups):
    copies = jnp.broadcast_to(shard[None], (len(groups[0]),) + shard.shape)
    return exchange(copies, groups)


def collected(chunks, groups):
    return jnp.sum(exchange(chunks, groups).astype(F32), axis=0)


def dot_t(left, right):
    return lax.dot_general(left, right, (((1,), (1,)), ((), ())), preferred_element_type=F32)


def fill_pairs(ids, table):
    slots, = ids.shape
    pairs = table.shape[0] - 1
    for p in range(pairs):
        table[p] = packed(0, 0, FB_DEV, DBLOCKS, DBLOCKS)
    p = jnp.int32(-1)
    last = jnp.int32(-1)
    first = jnp.int32(0)
    first_c = jnp.int32(0)
    open_pair = jnp.bool_(False)
    for i in range(slots):
        q = ids[i]
        h = q // DBLOCKS
        c = q % DBLOCKS
        live = h < FB_DEV
        joins = jnp.logical_and(open_pair, h == last)
        p = jnp.where(joins, p, p + 1)
        first = jnp.where(joins, first, i)
        first_c = jnp.where(joins, first_c, c)
        table[jnp.where(live, p, pairs)] = packed(
            first, i, h, first_c, jnp.where(joins, c, DBLOCKS)
        )
        open_pair = jnp.logical_not(joins)
        last = h


def packed(a, b, h, ca, cb):
    return (((h * 64 + ca) * 64 + cb) * 64 + a) * 64 + b


def unpacked(word):
    return (word // 64) % 64, word % 64, word // 64**4, (word // 64**3) % 64, (word // 64**2) % 64


def layer_kernel(ids, g_ref, wg_ref, wu_ref, wd_ref, out_ref, table, xs, ds, gu, dh, hid, dgu, fo, bo):
    rows, width = g_ref.shape
    half = rows // 2
    pairs = table.shape[0] - 1
    fill_pairs(ids, table)

    row = lax.broadcasted_iota(jnp.int32, (rows, rows), 0)
    col = lax.broadcasted_iota(jnp.int32, (rows, rows), 1)

    def source(i):
        within = i % half
        return (within // ROWS) * (2 * ROWS) + within % ROWS + (i // half) * ROWS

    sort_rows = (col == source(row)).astype(BF16)
    mix_rows = (row == source(col)).astype(BF16)

    gu[...] = jnp.zeros_like(gu)
    dh[...] = jnp.zeros_like(dh)
    fo[...] = jnp.zeros_like(fo)
    bo[...] = jnp.zeros_like(bo)
    for k in range(width // (2 * BLK)):
        part = jnp.dot(
            sort_rows, g_ref[:, k * 2 * BLK : (k + 1) * 2 * BLK], preferred_element_type=F32
        ).astype(BF16)
        for i in range(2):
            xs[2 * k + i] = part[:half, i * BLK : (i + 1) * BLK]
            ds[2 * k + i] = part[half:, i * BLK : (i + 1) * BLK]
    xs[DBLOCKS] = jnp.zeros((half, BLK), BF16)
    ds[DBLOCKS] = jnp.zeros((half, BLK), BF16)

    def tiles(ref, a, b, axis):
        return jnp.concatenate([ref[a], ref[b]], axis=axis)

    def both(a, b):
        return jnp.concatenate([tiles(wg_ref, a, b, 0), tiles(wu_ref, a, b, 0)], axis=1)

    for p in range(pairs):
        a, b, h, ca, cb = unpacked(table[p])
        gu[h] += jnp.dot(tiles(xs, ca, cb, 1), both(a, b), preferred_element_type=F32)
        dh[h] += dot_t(tiles(ds, ca, cb, 1), tiles(wd_ref, a, b, 1))

    for h in range(FB_DEV):
        gate = gu[h, :, :BLK]
        up = gu[h, :, BLK:]
        sig = 1.0 / (1.0 + jnp.exp(-gate))
        hid[h] = (gate * sig * up).astype(BF16)
        d_hidden = dh[h]
        dgu[h, :, :BLK] = (d_hidden * up * sig * (1.0 + gate * (1.0 - sig))).astype(BF16)
        dgu[h, :, BLK:] = (d_hidden * gate * sig).astype(BF16)
    hid[FB_DEV] = jnp.zeros((half, BLK), BF16)
    dgu[FB_DEV] = jnp.zeros((half, 2 * BLK), BF16)

    for p in range(pairs):
        a, b, h, ca, cb = unpacked(table[p])
        forth = jnp.dot(hid[h], tiles(wd_ref, a, b, 1), preferred_element_type=F32)
        back = dot_t(dgu[h], both(a, b))
        fo[ca] += forth[:, :BLK]
        fo[cb] += forth[:, BLK:]
        bo[ca] += back[:, :BLK]
        bo[cb] += back[:, BLK:]

    for k in range(DBLOCKS // 2):
        terms = [
            jnp.concatenate([fo[i].astype(BF16), bo[i].astype(BF16)], axis=0)
            for i in (2 * k, 2 * k + 1)
        ]
        out_ref[:, k * 2 * BLK : (k + 1) * 2 * BLK] = jnp.dot(
            mix_rows, jnp.concatenate(terms, axis=1), preferred_element_type=F32
        ).astype(BF16)


def layer(ids, gathered, w_gate, w_up, w_down):
    rows, width = gathered.shape
    half = rows // 2
    dblocks = width // BLK
    vmem = pl.BlockSpec(memory_space=pltpu.VMEM)
    slots = w_gate.shape[0]
    return pl.pallas_call(
        layer_kernel,
        out_shape=jax.ShapeDtypeStruct((rows, width), BF16),
        in_specs=[pl.BlockSpec(memory_space=pltpu.SMEM), vmem, vmem, vmem, vmem],
        out_specs=vmem,
        scratch_shapes=[
            pltpu.SMEM(((slots + FB_DEV) // 2 + 1,), jnp.int32),
            pltpu.VMEM((dblocks + 1, half, BLK), BF16),
            pltpu.VMEM((dblocks + 1, half, BLK), BF16),
            pltpu.VMEM((FB_DEV + 1, half, 2 * BLK), F32),
            pltpu.VMEM((FB_DEV + 1, half, BLK), F32),
            pltpu.VMEM((FB_DEV + 1, half, BLK), BF16),
            pltpu.VMEM((FB_DEV + 1, half, 2 * BLK), BF16),
            pltpu.VMEM((dblocks + 1, half, BLK), F32),
            pltpu.VMEM((dblocks + 1, half, BLK), F32),
        ],
        compiler_params=pltpu.CompilerParams(vmem_limit_bytes=40 * 1024 * 1024),
        cost_estimate=pl.CostEstimate(
            flops=12 * slots * half * BLK * BLK,
            bytes_accessed=6 * slots * BLK * BLK + 4 * rows * width,
            transcendentals=FB_DEV * half * BLK,
        ),
    )(ids, gathered, w_gate, w_up, w_down)


def on_device(carry_in, norm_gain, w_gate, w_up, w_down, tile_list, grad_in):
    _, batches, tok_dev, width = carry_in.shape
    own = batches * tok_dev
    carried = shifted(carry_in, "section", 1)
    dy_own, gain = lax.optimization_barrier(
        (grad_in.reshape(own, width), jnp.broadcast_to(norm_gain, (own, width)))
    )
    x_own = lax.optimization_barrier(carried.reshape(own, width)).astype(F32)
    scale = rms_scale(x_own)
    normed = (x_own * scale * gain).astype(BF16)

    shard = jnp.concatenate([normed, dy_own], axis=0)
    gathered = spread(shard, SPARSE).reshape(-1, width)
    gathered = spread(gathered, DENSE).reshape(-1, width)

    terms = layer(tile_list[0], gathered, w_gate[0], w_up[0], w_down[0])

    sums = collected(terms.reshape(len(DENSE[0]), -1, width), DENSE).astype(BF16)
    sums = collected(sums.reshape(len(SPARSE[0]), -1, width), SPARSE)
    ffn_own = sums[:own]
    grad_normed = sums[own:]

    section_out = (x_own + ffn_own).astype(BF16)
    mixed = jnp.mean(x_own * gain * grad_normed, axis=-1, keepdims=True)
    grad_x = dy_own.astype(F32) + scale * gain * grad_normed - x_own * scale**3 * mixed
    grad_back = shifted(grad_x.astype(BF16), "section", -1)
    return (
        section_out.reshape(1, batches, tok_dev, width),
        grad_back.reshape(1, batches, tok_dev, width),
    )


def solution(mesh):
    placed = (
        P("section", None, "tensor", None),
        P("section", None),
        P("section", "tensor", None, None),
        P("section", "tensor", None, None),
        P("section", "tensor", None, None),
        P("section", "tensor"),
        P("section", None, "tensor", None),
    )
    return jax.shard_map(
        on_device,
        mesh=mesh,
        in_specs=placed,
        out_specs=(P("section", None, "tensor", None), P("section", None, "tensor", None)),
        check_vma=False,
    )
```
